512 devices in a mesh: rep: 8 (over y_hi, core), ep: 64 (over y_lo, z, x).
Axes of the slice: x: 4, y: 8 (y_hi: 4, y_lo: 2; y = y_hi * 2 + y_lo), z: 8, core: 2. Of those that a mesh axis runs over, the one named last changes fastest.
Arguments:
- dense_grad: float32 [8, 64, 128, 7168], P('rep', 'ep'), may hold values from -16 to 16
- dense_param: float32 [128, 7168], P('ep'), may hold values from -5 to 5
- dense_first: float32 [128, 7168], P('ep'), may hold values from -128 to 128
- dense_second: float32 [128, 7168], P('ep'), may hold values from 20 to 2000
- expert_grad: float32 [8, 1024, 7168], P('rep', 'ep'), may hold values from -6 to 6
- expert_param: float32 [1024, 7168], P('ep'), may hold values from -5 to 5
- expert_first: float32 [1024, 7168], P('ep'), may hold values from -16 to 16
- expert_second: float32 [1024, 7168], P('ep'), may hold values from 0.5 to 50
Outputs:
- new_dense: float32 [128, 7168], replicated
- new_expert: float32 [1024, 7168], P('ep')
The draws below stay inside these ranges and needn't reach their ends.
All inputs are finite; a program needn't handle non-finite values.
Results may differ from the reference program's by a relative error of at most 0.00002.
Values sent between devices are 32-bit elements; how exact they have to be, the bound alone decides.
A program may use at most 64 MiB of HBM per device.

```python
import math
import jax
import jax.numpy as jnp
from jax import lax

D = 7168
ER = 16
DR = 128
EXPERTS = 64
N_REP = 8
N_EP = 64


def raised(entries, own_key, source, target, parts, factor):
    def block_of(position):
        return (jnp.arange(entries.shape[position]) // (entries.shape[position] // parts)).reshape((-1,) + (1,) * (entries.ndim - 1 - position))

    near = jax.random.permutation(own_key, parts)[block_of(target)]
    second = (block_of(target) + parts // 2) % parts
    return jnp.where((block_of(source) == near) | (block_of(source) == second), factor * entries, entries)


def steps_of(own_key, dims, pieces, low, top_value):
    factor_of = 1.0
    for dim, parts in pieces:
        heights = jax.random.uniform(jax.random.fold_in(jax.random.fold_in(own_key, 6), dim), (parts,), jnp.float32, low / len(pieces), top_value / len(pieces))
        factor_of = factor_of * jnp.repeat(jnp.exp(heights), dims[dim] // parts).reshape((-1,) + (1,) * (len(dims) - 1 - dim))
    return factor_of


def noise(rng, dims, deviation, bound, shards=(), held_as=jnp.bfloat16):
    factor_of = steps_of(rng, dims, shards, -0.22, 0.18) if shards else 1.0
    values = jax.random.normal(rng, dims, jnp.float32) * deviation * factor_of
    return jnp.minimum(jnp.maximum(values, -bound), bound).astype(held_as)


def gaussian_with(stream_key, extent, spread, most, pieces, heavy, held_as=jnp.bfloat16):
    values = spread * jax.random.normal(stream_key, extent, jnp.float32)
    if pieces:
        values = values * steps_of(stream_key, extent, pieces, -0.22, 0.18)
    return jnp.clip(raised(values, jax.random.fold_in(stream_key, 3), *heavy), -most, most).astype(held_as)


def setup_inputs(seed: int = 0) -> dict:
    arg_keys = jax.random.split(jax.random.key(seed), 9)
    return {
        "dense_grad": gaussian_with(arg_keys[0], (N_REP, N_EP, DR, D), 1.0, 16.0, ((0, 8), (1, 64)), (1, 2, 64, 4.0), jnp.float32),
        "dense_param": noise(arg_keys[1], (DR, D), 1.0, 5.0, ((0, 64),), jnp.float32),
        "dense_first": noise(arg_keys[2], (DR, D), 20.0, 128.0, ((0, 64),), jnp.float32),
        "dense_second": jnp.clip(jnp.exp(math.log(2000.0) - 4.6051702 * jax.random.uniform(arg_keys[3], (DR, D), jnp.float32) ** steps_of(arg_keys[3], (DR, D), ((0, 64),), -0.2, 0.2)), 20.0, 2000.0),
        "expert_grad": noise(arg_keys[4], (N_REP, EXPERTS * ER, D), 1.0, 6.0, ((0, 8), (1, 64)), jnp.float32),
        "expert_param": noise(arg_keys[5], (EXPERTS * ER, D), 1.0, 5.0, ((0, 64),), jnp.float32),
        "expert_first": noise(arg_keys[6], (EXPERTS * ER, D), 3.0, 16.0, ((0, 64),), jnp.float32),
        "expert_second": jnp.clip(jnp.exp(math.log(50.0) - 4.6051702 * jax.random.uniform(arg_keys[7], (EXPERTS * ER, D), jnp.float32) ** steps_of(arg_keys[7], (EXPERTS * ER, D), ((0, 64),), -0.2, 0.2)), 0.5, 50.0),
    }


beta_one = 0.9
beta_two = 0.95
corr_one = 0.19
corr_two = 0.0975
learn_rate = 0.2
decay_rate = 0.1
epsilon = 1e-08

def adamw(grad, param, first, second):
    first_new = beta_one * first + (1.0 - beta_one) * grad
    second_new = beta_two * second + (1.0 - beta_two) * grad * grad
    step_dir = first_new / corr_one / (jnp.sqrt(second_new / corr_two) + epsilon)
    return param - learn_rate * (step_dir + decay_rate * param)

def reference(dense_grad, dense_param, dense_first, dense_second, expert_grad, expert_param, expert_first, expert_second):
    dense_total = lax.optimization_barrier(jnp.sum(dense_grad, axis=(0, 1), dtype=jnp.float32))
    expert_total = lax.optimization_barrier(jnp.sum(expert_grad, axis=0, dtype=jnp.float32))
    new_dense = adamw(dense_total, dense_param, dense_first, dense_second)
    new_expert = adamw(expert_total, expert_param, expert_first, expert_second)
    return (new_dense, new_expert)
```

```python
import jax
import jax.numpy as jnp
from jax import lax
from jax.experimental import pallas as pl
from jax.experimental.pallas import tpu as pltpu
from jax.sharding import PartitionSpec as P

MESH = pl.DeviceIdType.MESH
D = 7168
T = 128


def adamw(grad, param, first, second):
    first_new = 0.9 * first + (1.0 - 0.9) * grad
    second_new = 0.95 * second + (1.0 - 0.95) * grad * grad
    step_dir = first_new / 0.19 / (jnp.sqrt(second_new / 0.0975) + 1e-08)
    return param - 0.2 * (step_dir + 0.1 * param)


def tiles(start, count):
    first = start * T
    if not isinstance(first, int):
        first = pl.multiple_of(first, T)
    return pl.ds(first, count * T)


def eight(index):
    return pl.ds(pl.multiple_of(index * 8, 8), 8)


def kernel(
    grad, param, first, second, egrad, eparam, efirst, esecond,
    out, eout,
    g_a, p_a, g_c, p_c, g_b, p_b, g_e, p_e,
    r_a1, s_a, r_a2y, t_ay, r_a2z, t_az, r_a3,
    r_c1, s_c, r_c2, t_c, r_c3,
    r_b1, s_b, r_b2, t_b, r_b3,
    r_e, ep_buf, state, gathered, packed,
    load_sem, send_sem, recv_sem,
):
    rep, ep = lax.axis_index("rep"), lax.axis_index("ep")
    core = lax.rem(rep, 2)
    x, z = lax.rem(ep, 4), lax.rem(ep // 4, 8)
    yh, yl = rep // 2, ep // 32
    y = yh * 2 + yl

    def at(xx, yy, zz, cc):
        return {"rep": (yy // 2) * 2 + cc, "ep": lax.rem(yy, 2) * 32 + zz * 4 + xx}

    def x_peer(d):
        return at(lax.rem(x + d, 4), y, z, core)

    def y_peer(d):
        return at(x, lax.rem(y + d, 8), z, core)

    def z_peer(d):
        return at(x, y, lax.rem(z + d, 8), core)

    partner = at(x, y, z, 1 - core)

    barrier = pltpu.get_barrier_semaphore()
    peers = [partner] + [x_peer(d) for d in range(1, 4)]
    peers += [f(d) for d in range(1, 8) for f in (y_peer, z_peer)]
    for peer in peers:
        pl.semaphore_signal(barrier, inc=1, device_id=peer, device_id_type=MESH)

    def body(c):
        n_load, n_sem = [0], [0]
        sent = []

        def load(src, dst):
            copy = pltpu.make_async_copy(src, dst, load_sem.at[n_load[0]])
            n_load[0] += 1
            copy.start()
            return copy

        def link(src, dst, device):
            k = n_sem[0]
            n_sem[0] += 1
            return pltpu.make_async_remote_copy(
                src, dst, send_sem.at[k], recv_sem.at[k], device_id=device, device_id_type=MESH
            )

        def send(src, dst, device):
            copy = link(src, dst, device)
            copy.start()
            sent.append(copy)
            return copy

        o = 1 - c
        order = [lax.rem(x + d, 4) for d in (2, 1, 3, 0)]
        own_a, own_c, own_b, own_e = [], None, None, None
        for xx in order:
            own_a.append(load(grad.at[:, :, tiles(c * 16 + xx * 4, 4)], g_a.at[xx]))
        own_c = load(grad.at[:, :, tiles(32 + c * 8, 8)], g_c)
        own_b = load(grad.at[:, :, tiles(48 + c * 4, 4)], g_b)
        own_e = load(egrad.at[:, tiles(c * 28, 28)], g_e)
        e_cols = tiles(c * 28 + yh * 7, 7)
        own_s = [load(r, state.at[i]) for i, r in enumerate((param, first, second))]
        own_ep = [load(r.at[:, e_cols], ep_buf.at[i]) for i, r in enumerate((eparam, efirst, esecond))]
        for copy in own_s:
            copy.wait()

        pl.semaphore_wait(barrier, len(peers))

        part_a = []
        for i, xx in enumerate(order):
            part_a.append(send(grad.at[:, :, tiles(o * 16 + xx * 4, 4)], p_a.at[xx], partner))
            if i == 0:
                part_c = send(grad.at[:, :, tiles(32 + o * 8, 8)], p_c, partner)
            if i == 1:
                part_b = send(grad.at[:, :, tiles(48 + o * 4, 4)], p_b, partner)
                part_e = send(egrad.at[:, tiles(o * 28, 28)], p_e, partner)

        def state_tiles(xx):
            jj = lax.rem(y, 4) // 2
            return (c * 16 + xx * 4 + yh, 32 + c * 8 + xx * 2 + jj, 48 + c * 4 + yh)

        state_recv = []
        for d in range(1, 4):
            for i, ct in enumerate(state_tiles(lax.rem(x + d, 4))):
                state_recv.append(send(state.at[:, :, tiles(ct, 1)], gathered.at[d, i], x_peer(d)))

        def piece(ref, p):
            if c == 0:
                return ref.at[lax.rem(p, 2), :, tiles(p // 2, 1)]
            return ref.at[:, eight(p), :]

        def a_send(i, xx, d):
            own_a[i].wait()
            part_a[i].wait_recv()
            g_a[xx] = g_a[xx] + p_a[xx]
            if d == 0:
                return None
            mid = y if c == 0 else z
            return [
                send(piece(g_a.at[xx], lax.rem(mid + k, 8)), piece(r_a1.at[d - 1], lax.rem(mid + k, 8)), x_peer(d))
                for k in range(8)
            ]

        a1 = {}
        a1[2] = a_send(0, order[0], 2)

        own_c.wait()
        part_c.wait_recv()
        g_c[...] = g_c[...] + p_c[...]
        c1 = [
            send(g_c.at[:, eight(lax.rem(z + d, 8)), :], r_c1.at[d - 1], z_peer(d)) for d in range(1, 8)
        ]

        a1[1] = a_send(1, order[1], 1)

        own_b.wait()
        part_b.wait_recv()
        g_b[...] = g_b[...] + p_b[...]
        b1 = []
        for d in range(1, 8):
            yy = lax.rem(y + d, 8)
            b1.append(send(g_b.at[lax.rem(yy, 2), :, tiles(yy // 2, 1)], r_b1.at[d - 1], y_peer(d)))

        own_e.wait()
        part_e.wait_recv()
        g_e[...] = g_e[...] + p_e[...]
        e1 = [
            send(g_e.at[:, tiles(lax.rem(yh + d, 4) * 7, 7)], r_e.at[d - 1], y_peer(2 * d)) for d in range(1, 4)
        ]

        a1[3] = a_send(2, order[2], 3)
        a_send(3, order[3], 0)

        for copy in state_recv:
            copy.wait_recv()
        for i, ct in enumerate(state_tiles(x)):
            for d in range(4):
                row = pl.ds(2 * lax.rem(x + 4 - d, 4), 2)
                for j in range(3):
                    if d == 0:
                        packed[i, j, row, :] = state[j, :, tiles(ct, 1)]
                    else:
                        packed[i, j, row, :] = gathered[d, i, j]

        mid = y if c == 0 else z
        second_a, r_a2, t_a = ([], r_a2y, t_ay) if c == 0 else ([], r_a2z, t_az)
        mid_peer, last_peer = (y_peer, z_peer) if c == 0 else (z_peer, y_peer)
        for k in (1, 2, 3, 4, 5, 6, 7, 0):
            p = lax.rem(mid + k, 8)
            for d in (2, 1, 3):
                a1[d][k].wait_recv()
            total = piece(g_a.at[x], p)[...]
            for d in (1, 2, 3):
                total = total + piece(r_a1.at[d - 1], p)[...]
            if k:
                piece(s_a, p)[...] = total
                second_a.append(send(piece(s_a, p), r_a2.at[k - 1], mid_peer(k)))
            else:
                t_a[...] = total

        for copy in c1:
            copy.wait_recv()
        total = g_c[:, eight(z), :]
        for d in range(1, 8):
            total = total + r_c1[d - 1]
        s_c[...] = total
        c2 = [
            send(s_c.at[:, :, tiles(2 * lax.rem(x + d, 4), 2)], r_c2.at[d - 1], x_peer(d)) for d in range(1, 4)
        ]

        for copy in b1:
            copy.wait_recv()
        total = g_b[yl, :, tiles(yh, 1)]
        for d in range(1, 8):
            total = total + r_b1[d - 1]
        s_b[...] = total
        b2 = [send(s_b.at[eight(lax.rem(z + d, 8)), :], r_b2.at[d - 1], z_peer(d)) for d in range(1, 8)]

        for copy in e1:
            copy.wait_recv()
        for copy in own_ep:
            copy.wait()
        total = g_e[:, tiles(yh * 7, 7)]
        for d in range(1, 4):
            total = total + r_e[d - 1]
        eout[:, e_cols] = adamw(total, ep_buf[0], ep_buf[1], ep_buf[2])
        e2 = [send(eout.at[:, e_cols], eout.at[:, e_cols], y_peer(2 * d)) for d in range(1, 4)]
        e_done = [send(eout.at[:, e_cols], eout.at[:, e_cols], partner)]

        for copy in second_a:
            copy.wait_recv()
        total = t_a[...]
        for d in range(1, 8):
            total = total + r_a2[d - 1]
        t_a[...] = total
        a3 = []
        for d in range(1, 8):
            if c == 0:
                src = t_a.at[eight(lax.rem(z + d, 8)), :]
            else:
                yy = lax.rem(y + d, 8)
                src = t_a.at[lax.rem(yy, 2), :, tiles(yy // 2, 1)]
            a3.append(send(src, r_a3.at[d - 1], last_peer(d)))

        for copy in c2:
            copy.wait_recv()
        total = s_c[:, :, tiles(2 * x, 2)]
        for d in range(1, 4):
            total = total + r_c2[d - 1]
        t_c[...] = total
        c_first = 4 * lax.rem(x, 2)

        def c_owner(d):
            yy = lax.rem(y + d, 8)
            return yy // 4 == lax.rem(x, 2), yy

        c3 = []
        for d in range(1, 8):
            owns, yy = c_owner(d)
            copy = link(t_c.at[lax.rem(yy, 2), :, tiles(lax.rem(yy, 4) // 2, 1)], r_c3.at[d - 1], y_peer(d))
            c3.append(copy)

            @pl.when(owns)
            def _(copy=copy):
                copy.start()

        for copy in b2:
            copy.wait_recv()
        total = s_b[eight(z), :]
        for d in range(1, 8):
            total = total + r_b2[d - 1]
        t_b[...] = total
        b3 = []
        for d in range(1, 4):
            copy = link(t_b, r_b3.at[d - 1], x_peer(d))
            b3.append(copy)

            @pl.when(lax.rem(x + d, 4) == yh)
            def _(copy=copy):
                copy.start()

        for copy in a3:
            copy.wait_recv()
        total = t_a[eight(z), :] if c == 0 else t_a[yl, :, tiles(yh, 1)]
        for d in range(1, 8):
            total = total + r_a3[d - 1]
        ct_a, ct_c, ct_b = state_tiles(x)
        tile_a = out.at[yl, eight(z), tiles(ct_a, 1)]
        tile_a[...] = adamw(total, packed[0, 0], packed[0, 1], packed[0, 2])
        a4 = [send(tile_a, tile_a, last_peer(d)) for d in range(1, 8)]

        tile_c = out.at[yl, eight(z), tiles(ct_c, 1)]
        c4 = [link(tile_c, tile_c, y_peer(d)) for d in range(1, 8)]
        mine_c = y // 4 == lax.rem(x, 2)

        @pl.when(mine_c)
        def _():
            for copy in c3:
                copy.wait_recv()
            total = t_c[yl, :, tiles(lax.rem(y, 4) // 2, 1)]
            for d in range(1, 8):
                total = total + r_c3[d - 1]
            tile_c[...] = adamw(total, packed[1, 0], packed[1, 1], packed[1, 2])
            for copy in c4:
                copy.start()

        tile_b = out.at[yl, eight(z), tiles(ct_b, 1)]
        b4 = [link(tile_b, tile_b, x_peer(d)) for d in range(1, 4)]
        mine_b = x == yh

        @pl.when(mine_b)
        def _():
            for copy in b3:
                copy.wait_recv()
            total = t_b[...]
            for d in range(1, 4):
                total = total + r_b3[d - 1]
            tile_b[...] = adamw(total, packed[2, 0], packed[2, 1], packed[2, 2])
            for copy in b4:
                copy.start()

        for d in range(1, 4):
            e2[d - 1].wait_recv()
            cols = tiles(c * 28 + lax.rem(yh + 4 - d, 4) * 7, 7)
            e_done.append(send(eout.at[:, cols], eout.at[:, cols], partner))

        for copy in a4:
            copy.wait_recv()
        block_a = out.at[:, :, tiles(c * 16 + x * 4, 4)]
        mine = piece(block_a, mid)
        a5 = [send(mine, mine, mid_peer(d)) for d in range(1, 8)]
        done = []
        a6 = {1: [], 2: [], 3: []}
        for d in (2, 1, 3):
            a6[d].append(send(mine, mine, x_peer(d)))
        done.append(send(mine, mine, partner))

        for d in range(1, 4):
            @pl.when(lax.rem(x + 4 - d, 4) == yh)
            def _(copy=b4[d - 1]):
                copy.wait_recv()
        b5 = [send(tile_b, tile_b, z_peer(d)) for d in range(1, 8)]

        for d in range(1, 8):
            @pl.when(lax.rem(y + 8 - d, 8) // 4 == lax.rem(x, 2))
            def _(copy=c4[d - 1]):
                copy.wait_recv()
        block_c = out.at[:, eight(z), tiles(32 + c * 8 + x * 2, 2)]
        c5 = [send(block_c, block_c, x_peer(d)) for d in range(1, 4)]

        for copy in b5:
            copy.wait_recv()
        col_b = out.at[yl, :, tiles(ct_b, 1)]
        b6 = [send(col_b, col_b, y_peer(d)) for d in range(1, 8)]

        for copy in c5:
            copy.wait_recv()
        row_c = out.at[:, eight(z), tiles(32 + c * 8, 8)]
        c6 = [send(row_c, row_c, z_peer(d)) for d in range(1, 8)]

        for k in range(1, 8):
            a5[k - 1].wait_recv()
            got = piece(block_a, lax.rem(mid + 8 - k, 8))
            for d in (2, 1, 3):
                a6[d].append(send(got, got, x_peer(d)))
            done.append(send(got, got, partner))

        for copy in b6:
            copy.wait_recv()
        all_b = out.at[:, :, tiles(48 + c * 4, 4)]
        done.append(send(all_b, all_b, partner))
        for k in range(8):
            for d in (1, 3, 2):
                a6[d][k].wait_recv()
                got = piece(out.at[:, :, tiles(c * 16 + lax.rem(x + 4 - d, 4) * 4, 4)], lax.rem(mid + 8 - k, 8))
                done.append(send(got, got, partner))
        for copy in c6:
            copy.wait_recv()
        all_c = out.at[:, :, tiles(32 + c * 8, 8)]
        done.append(send(all_c, all_c, partner))

        for copy in e_done + done:
            copy.wait_recv()
        for copy in sent:
            copy.wait_send()
        for d in range(1, 8):
            @pl.when(c_owner(d)[0])
            def _(copy=c3[d - 1]):
                copy.wait_send()
        for d in range(1, 4):
            @pl.when(lax.rem(x + d, 4) == yh)
            def _(copy=b3[d - 1]):
                copy.wait_send()

        @pl.when(mine_c)
        def _():
            for copy in c4:
                copy.wait_send()

        @pl.when(mine_b)
        def _():
            for copy in b4:
                copy.wait_send()

    for value in range(2):
        @pl.when(core == value)
        def _(value=value):
            body(value)


def shards(grad, param, first, second, egrad, eparam, efirst, esecond):
    vmem = lambda *shape: pltpu.VMEM(shape, jnp.float32)
    block = (2, 64, 4 * T)
    out, eout = pl.pallas_call(
        kernel,
        out_shape=(
            jax.ShapeDtypeStruct((2, 64, D), jnp.float32),
            jax.ShapeDtypeStruct((16, D), jnp.float32),
        ),
        in_specs=[pl.BlockSpec(memory_space=pl.ANY)] * 8,
        out_specs=(pl.BlockSpec(memory_space=pltpu.VMEM),) * 2,
        scratch_shapes=[
            vmem(4, *block), vmem(4, *block), vmem(2, 64, 8 * T), vmem(2, 64, 8 * T), vmem(*block), vmem(*block),
            vmem(16, 28 * T), vmem(16, 28 * T),
            vmem(3, *block), vmem(*block), vmem(7, 64, T), vmem(64, T), vmem(7, 2, 8, 4 * T), vmem(2, 8, 4 * T), vmem(7, 8, T),
            vmem(7, 2, 8, 8 * T), vmem(2, 8, 8 * T), vmem(3, 2, 8, 2 * T), vmem(2, 8, 2 * T), vmem(7, 8, T),
            vmem(7, 64, T), vmem(64, T), vmem(7, 8, T), vmem(8, T), vmem(3, 8, T),
            vmem(3, 16, 7 * T), vmem(3, 16, 7 * T), vmem(3, 2, D), vmem(4, 3, 3, 2, T), vmem(3, 3, 8, T),
            pltpu.SemaphoreType.DMA((16,)),
            pltpu.SemaphoreType.DMA((240,)),
            pltpu.SemaphoreType.DMA((240,)),
        ],
        compiler_params=pltpu.CompilerParams(
            collective_id=0, has_side_effects=True, vmem_limit_bytes=40 * 1024 * 1024
        ),
        name="reduce_update_gather",
    )(
        grad.reshape(2, 64, D), param, first, second,
        egrad.reshape(16, D), eparam, efirst, esecond,
    )
    return out.reshape(128, D), eout


def solution(mesh):
    placed = (
        P("rep", "ep", None, None),
        P("ep", None),
        P("ep", None),
        P("ep", None),
        P("rep", "ep", None),
        P("ep", None),
        P("ep", None),
        P("ep", None),
    )
    return jax.shard_map(
        shards, mesh=mesh, in_specs=placed, out_specs=(P(), P("ep", None)), check_vma=False
    )
```

```python
import jax
import jax.numpy as jnp
from jax import lax
from jax.experimental import pallas as pl
from jax.experimental.pallas import tpu as pltpu
from jax.sharding import PartitionSpec as P

MESH = pl.DeviceIdType.MESH
D = 7168
T = 128
ORDER = (4, 3, 5, 2, 6, 1, 7, 0)
DIRECT = (3, 4)


def way(k):
    return 1 if k in (0, 1, 2, 3) else 3


class Reduce:
    def __init__(self, part, half, relays, arrived, send, peer):
        self.part, self.half, self.relays, self.arrived = part, half, relays, arrived
        self.send, self.peer = send, peer

    def start(self):
        part, half, peer, relays = self.part, self.half, self.peer, self.relays
        self.three = [self.send(part(3), relays.at[0], peer(1)), self.send(part(-3), relays.at[1], peer(7))]
        self.four = [
            self.send(half(part(4), i), half(relays.at[2], i), peer((2, 6)[i])) for i in range(2)
        ]
        self.one = [self.send(part(d), self.arrived.at[i], peer(d)) for i, d in enumerate((1, 7))]

    def relay(self):
        self.two = []
        for i, d in enumerate((2, 6)):
            mine = self.part(d)
            self.three[i].wait_recv()
            mine[...] = mine[...] + self.relays[i]
            self.four[i].wait_recv()
            more = self.half(mine, i)
            more[...] = more[...] + self.half(self.relays.at[2], i)[...]
            self.two.append(self.send(mine, self.arrived.at[2 + i], self.peer(d)))

    def finish(self):
        total = self.part(0)[...]
        for i, copy in enumerate(self.one + self.two):
            copy.wait_recv()
            total = total + self.arrived[i]
        return total


class Gather:
    def __init__(self, block, half, send, peer):
        self.block, self.half, self.send, self.peer = block, half, send, peer

    def start(self):
        mine = self.block(0)
        self.two = [self.send(mine, mine, self.peer(d)) for d in (2, 6)]
        self.one = [self.send(mine, mine, self.peer(d)) for d in (1, 7)]

    def forward(self):
        self.rest = []
        for i, d in enumerate((2, 6)):
            self.two[i].wait_recv()
            got = self.block(-d)
            self.rest.append(self.send(got, got, self.peer((1, 7)[i])))
            self.rest.append(self.send(self.half(got, i), self.half(got, i), self.peer(d)))

    def finish(self):
        for copy in self.one + self.rest:
            copy.wait_recv()


def adamw(grad, param, first, second):
    first_new = 0.9 * first + (1.0 - 0.9) * grad
    second_new = 0.95 * second + (1.0 - 0.95) * grad * grad
    step_dir = first_new / 0.19 / (jnp.sqrt(second_new / 0.0975) + 1e-08)
    return param - 0.2 * (step_dir + 0.1 * param)


def tiles(start, count):
    first = start * T
    if not isinstance(first, int):
        first = pl.multiple_of(first, T)
    return pl.ds(first, count * T)


def eight(index):
    return pl.ds(pl.multiple_of(index * 8, 8), 8)


def kernel(
    grad, param, first, second, egrad, eparam, efirst, esecond,
    out, eout,
    g_a, p_a, g_c, p_c, g_b, p_b, g_e, p_e,
    r_a1, relay_a, s_a, r_a2y, t_ay, r_a2z, t_az, r_a3,
    r_c1, relay_c, s_c, r_c2, t_c, r_c3,
    r_b1, relay_b, s_b, r_b2, r_b3,
    r_e, ep_buf, state, gathered, packed,
    load_sem, send_sem, recv_sem,
):
    rep, ep = lax.axis_index("rep"), lax.axis_index("ep")
    yh, yl = rep // 2, ep // 32
    core = rep - yh * 2
    rest = ep - yl * 32
    z = rest // 4
    x = rest - z * 4
    y = yh * 2 + yl

    def around(v, n):
        return [v] + [jnp.where(v + d >= n, v + d - n, v + d) for d in range(1, n)]

    xs, ys, zs = around(x, 4), around(y, 8), around(z, 8)
    yhs = [v // 2 for v in ys]
    yls = [yl, 1 - yl] * 4

    def x_peer(d):
        return {"rep": rep, "ep": ep + (xs[d] - x)}

    def y_peer(d):
        return {"rep": yhs[d] * 2 + core, "ep": ep + (yls[d] - yl) * 32}

    def z_peer(d):
        return {"rep": rep, "ep": ep + (zs[d] - z) * 4}

    partner = {"rep": rep + 1 - 2 * core, "ep": ep}

    barrier = pltpu.get_barrier_semaphore()
    peers = [f(d) for d in (4, 3, 5, 2, 6, 1, 7) for f in (y_peer, z_peer)]
    peers += [x_peer(d) for d in (2, 1, 3)] + [partner]
    for peer in peers:
        pl.semaphore_signal(barrier, inc=1, device_id=peer, device_id_type=MESH)

    def body(c):
        n_load, n_sem = [0], [0]
        sent, flushed = [], [0]

        def load(src, dst):
            copy = pltpu.make_async_copy(src, dst, load_sem.at[n_load[0]])
            n_load[0] += 1
            copy.start()
            return copy

        def link(src, dst, device):
            k = n_sem[0]
            n_sem[0] += 1
            return pltpu.make_async_remote_copy(
                src, dst, send_sem.at[k], recv_sem.at[k], device_id=device, device_id_type=MESH
            )

        def flush():
            for copy in sent[flushed[0]:]:
                copy.wait_send()
            flushed[0] = len(sent)

        def send(src, dst, device):
            copy = link(src, dst, device)
            copy.start()
            sent.append(copy)
            return copy

        o = 1 - c
        order = [xs[d] for d in (2, 1, 3, 0)]
        own_a = [load(grad.at[:, :, tiles(c * 16 + xx * 4, 4)], g_a.at[xx]) for xx in order]
        own_c = load(grad.at[:, :, tiles(32 + c * 8, 8)], g_c)
        own_b = load(grad.at[:, :, tiles(48 + c * 4, 4)], g_b)
        own_e = load(egrad.at[:, tiles(c * 28, 28)], g_e)
        e_cols = tiles(c * 28 + yh * 7, 7)
        own_s = [load(r, state.at[i]) for i, r in enumerate((param, first, second))]
        own_ep = [load(r.at[:, e_cols], ep_buf.at[i]) for i, r in enumerate((eparam, efirst, esecond))]
        for copy in own_s:
            copy.wait()

        pl.semaphore_wait(barrier, len(peers))

        def part(xx):
            return send(grad.at[:, :, tiles(o * 16 + xx * 4, 4)], p_a.at[xx], partner)

        part_a = [part(order[0])]
        part_c = send(grad.at[:, :, tiles(32 + o * 8, 8)], p_c, partner)
        part_b = send(grad.at[:, :, tiles(48 + o * 4, 4)], p_b, partner)
        part_e = send(egrad.at[:, tiles(o * 28, 28)], p_e, partner)
        part_a += [part(xx) for xx in order[1:]]

        def state_tiles(xx):
            jj = jnp.where(yh >= 2, yh - 2, yh)
            return (c * 16 + xx * 4 + yh, 32 + c * 8 + xx * 2 + jj, 48 + c * 4 + yh)

        state_recv = []
        for d in range(1, 4):
            for i, ct in enumerate(state_tiles(xs[d])):
                state_recv.append(send(state.at[:, :, tiles(ct, 1)], gathered.at[d, i], x_peer(d)))

        def piece(ref, k):
            k = k % 8
            if c == 0:
                return ref.at[yls[k], :, tiles(yhs[k], 1)]
            return ref.at[:, eight(zs[k]), :]

        def a_sum(i):
            own_a[i].wait()
            part_a[i].wait_recv()
            g_a[order[i]] = g_a[order[i]] + p_a[order[i]]

        a_sum(0)
        far = {k: send(piece(g_a.at[xs[2]], k), piece(relay_a, k), x_peer(way(k))) for k in ORDER}

        own_c.wait()
        part_c.wait_recv()
        g_c[...] = g_c[...] + p_c[...]
        ring_c = []
        for h in range(2):
            ring_c.append(
                Reduce(
                    lambda k, h=h: g_c.at[:, eight(zs[k % 8]), 4 * T * h : 4 * T * (h + 1)],
                    lambda ref, i: ref.at[i],
                    relay_c.at[h], r_c1.at[h], send, z_peer,
                )
            )
            ring_c[h].start()

        own_b.wait()
        part_b.wait_recv()
        g_b[...] = g_b[...] + p_b[...]
        ring_b = Reduce(
            lambda k: g_b.at[yls[k % 8], :, tiles(yhs[k % 8], 1)],
            lambda ref, i: ref.at[pl.ds(32 * i, 32), :],
            relay_b, r_b1, send, y_peer,
        )
        ring_b.start()

        own_e.wait()
        part_e.wait_recv()
        g_e[...] = g_e[...] + p_e[...]
        e1 = [
            send(g_e.at[:, tiles(yhs[2 * d] * 7, 7)], r_e.at[d - 1], y_peer(2 * d)) for d in range(1, 4)
        ]

        a_sum(1)
        a_sum(2)
        near = {1: {}, 3: {}}
        for k in ORDER:
            d = 4 - way(k)
            near[d][k] = send(piece(g_a.at[xs[d]], k), piece(r_a1.at[d // 2], k), x_peer(d))

        for k in ORDER:
            d = way(k)
            far[k].wait_recv()
            mine = piece(g_a.at[xs[d]], k)
            mine[...] = mine[...] + piece(relay_a, k)[...]
            near[d][k] = send(mine, piece(r_a1.at[d // 2], k), x_peer(d))

        ring_c[0].relay()
        ring_c[1].relay()
        ring_b.relay()
        a_sum(3)

        for copy in state_recv:
            copy.wait_recv()
        for i, ct in enumerate(state_tiles(x)):
            for d in range(4):
                row = pl.ds(2 * xs[(4 - d) % 4], 2)
                for j in range(3):
                    if d == 0:
                        packed[i, j, row, :] = state[j, :, tiles(ct, 1)]
                    else:
                        packed[i, j, row, :] = gathered[d, i, j]

        second_a, r_a2, t_a = ([], r_a2y, t_ay) if c == 0 else ([], r_a2z, t_az)
        mid_peer, last_peer = (y_peer, z_peer) if c == 0 else (z_peer, y_peer)
        for k in ORDER:
            near[1][k].wait_recv()
            near[3][k].wait_recv()
            total = piece(g_a.at[x], k)[...] + piece(r_a1.at[0], k)[...] + piece(r_a1.at[1], k)[...]
            if k:
                piece(s_a, k)[...] = total
                second_a.append(send(piece(s_a, k), r_a2.at[k - 1], mid_peer(k)))
            else:
                t_a[...] = total

        for h in range(2):
            s_c[:, :, 4 * T * h : 4 * T * (h + 1)] = ring_c[h].finish()
        c2 = [
            send(s_c.at[:, :, tiles(2 * xs[d], 2)], r_c2.at[d - 1], x_peer(d)) for d in (2, 1, 3)
        ]

        s_b[...] = ring_b.finish()
        b2 = [send(s_b.at[eight(zs[d]), :], r_b2.at[d - 1], z_peer(d)) for d in ORDER[:7]]

        for copy in e1:
            copy.wait_recv()
        for copy in own_ep:
            copy.wait()
        total = g_e[:, tiles(yh * 7, 7)]
        for d in range(1, 4):
            total = total + r_e[d - 1]
        eout[:, e_cols] = adamw(total, ep_buf[0], ep_buf[1], ep_buf[2])

        for copy in second_a:
            copy.wait_recv()
        total = t_a[...]
        for d in range(1, 8):
            total = total + r_a2[d - 1]
        t_a[...] = total
        a3 = []
        for d in ORDER[:7]:
            if c == 0:
                src = t_a.at[eight(zs[d]), :]
            else:
                src = t_a.at[yls[d], :, tiles(yhs[d], 1)]
            a3.append(send(src, r_a3.at[d - 1], last_peer(d)))

        for copy in c2:
            copy.wait_recv()
        total = s_c[:, :, tiles(2 * x, 2)]
        for d in range(1, 4):
            total = total + r_c2[d - 1]
        t_c[...] = total
        x_odd = x - 2 * (x // 2)
        halves = [v // 2 for v in yhs]
        owner = [v == x_odd for v in halves]

        c3 = []
        for d in range(1, 8):
            copy = link(t_c.at[yls[d], :, tiles(yhs[d] - 2 * halves[d], 1)], r_c3.at[d - 1], y_peer(d))
            c3.append(copy)

            @pl.when(owner[d])
            def _(copy=copy):
                copy.start()

        for copy in b2:
            copy.wait_recv()
        total = s_b[eight(z), :]
        for d in range(1, 8):
            total = total + r_b2[d - 1]
        r_b3[x] = total
        b3 = [send(r_b3.at[x], r_b3.at[x], x_peer(d)) for d in (2, 1, 3)]

        for copy in a3:
            copy.wait_recv()
        total = t_a[eight(z), :] if c == 0 else t_a[yl, :, tiles(yh, 1)]
        for d in range(1, 8):
            total = total + r_a3[d - 1]
        ct_a, ct_c, ct_b = state_tiles(x)
        tile_a = out.at[yl, eight(z), tiles(ct_a, 1)]
        tile_a[...] = adamw(total, packed[0, 0], packed[0, 1], packed[0, 2])
        a4 = [send(tile_a, tile_a, last_peer(d)) for d in ORDER[:7]]

        tile_c = out.at[yl, eight(z), tiles(ct_c, 1)]
        c4 = [link(tile_c, tile_c, y_peer(d)) for d in range(1, 8)]
        mine_c = owner[0]

        @pl.when(mine_c)
        def _():
            for copy in c3:
                copy.wait_recv()
            total = t_c[yl, :, tiles(yh - 2 * halves[0], 1)]
            for d in range(1, 8):
                total = total + r_c3[d - 1]
            tile_c[...] = adamw(total, packed[1, 0], packed[1, 1], packed[1, 2])
            for copy in c4:
                copy.start()

        tile_b = out.at[yl, eight(z), tiles(ct_b, 1)]
        for copy in b3:
            copy.wait_recv()
        total = r_b3[0] + r_b3[1] + r_b3[2] + r_b3[3]
        tile_b[...] = adamw(total, packed[2, 0], packed[2, 1], packed[2, 2])
        b5 = [send(tile_b, tile_b, z_peer(d)) for d in ORDER[:7]]

        for d in range(1, 8):
            @pl.when(owner[d])
            def _(copy=c3[d - 1]):
                copy.wait_send()

        flush()

        for copy in a4:
            copy.wait_recv()
        block_a = [out.at[:, :, tiles(c * 16 + xx * 4, 4)] for xx in xs]
        mine = piece(block_a[0], 0)
        a5 = {k: send(mine, mine, mid_peer(k)) for k in ORDER[:7]}
        done = []
        a6, a7 = {1: {}, 3: {}}, {}

        def a_out(q):
            got = piece(block_a[0], q)
            if q in DIRECT:
                a7[q] = send(got, got, x_peer(2))
            for d in (way(q), 4 - way(q)):
                a6[d][q] = send(got, got, x_peer(d))
            done.append(send(got, got, partner))

        def a_in(q):
            for d in (way(q), 4 - way(q)):
                a6[d][q].wait_recv()
                got = piece(block_a[4 - d], q)
                if q not in DIRECT and d == way(q):
                    a7[q] = send(got, got, x_peer(d))
                done.append(send(got, got, partner))

        def a_last(q):
            a7[q].wait_recv()
            got = piece(block_a[2], q)
            done.append(send(got, got, partner))

        a_out(0)

        for d in range(1, 8):
            @pl.when(owner[8 - d])
            def _(copy=c4[d - 1]):
                copy.wait_recv()
        mine = out.at[:, eight(z), tiles(32 + c * 8 + x * 2, 2)]
        c5 = {d: send(mine, mine, x_peer(d)) for d in (2, 1, 3)}
        c6 = [
            Gather(
                lambda k, xx=xx: out.at[:, eight(zs[k % 8]), tiles(32 + c * 8 + xx * 2, 2)],
                lambda ref, i: ref.at[i],
                send, z_peer,
            )
            for xx in xs
        ]
        c6[0].start()

        def c_in(d):
            c5[d].wait_recv()
            c6[4 - d].start()

        def c_last(i):
            c6[i].finish()
            got = out.at[:, :, tiles(32 + c * 8 + xs[i] * 2, 2)]
            done.append(send(got, got, partner))

        for copy in b5:
            copy.wait_recv()
        b6 = Gather(
            lambda k: out.at[yls[k % 8], :, tiles(48 + c * 4 + yhs[k % 8], 1)],
            lambda ref, i: ref.at[pl.ds(32 * i, 32), :],
            send, y_peer,
        )
        b6.start()

        e2 = [send(eout.at[:, e_cols], eout.at[:, e_cols], y_peer(2 * d)) for d in range(1, 4)]
        done.append(send(eout.at[:, e_cols], eout.at[:, e_cols], partner))

        def e_in(d):
            e2[d - 1].wait_recv()
            cols = tiles(c * 28 + yhs[8 - 2 * d] * 7, 7)
            done.append(send(eout.at[:, cols], eout.at[:, cols], partner))

        def a_mid(q):
            a5[8 - q].wait_recv()
            a_out(q)

        a_mid(7)
        a_mid(1)
        a_in(0)
        c_in(1)
        c_in(3)
        a_mid(6)
        a_mid(2)
        c_in(2)
        c6[0].forward()
        b6.forward()
        a_mid(5)
        a_mid(3)
        a_mid(4)
        a_in(7)
        a_in(1)
        c6[3].forward()
        c6[1].forward()
        a_last(0)
        a_in(6)
        a_in(2)
        c6[2].forward()
        b6.finish()
        got = out.at[:, :, tiles(48 + c * 4, 4)]
        done.append(send(got, got, partner))

        @pl.when(mine_c)
        def _():
            for copy in c4:
                copy.wait_send()

        a_last(7)
        a_last(1)
        e_in(1)
        e_in(2)
        e_in(3)
        c_last(0)
        a_in(5)
        a_in(3)
        a_in(4)
        c_last(3)
        c_last(1)
        a_last(6)
        a_last(2)
        a_last(5)
        a_last(3)
        a_last(4)
        c_last(2)

        flush()
        for copy in done:
            copy.wait_recv()

    for value in range(2):
        @pl.when(core == value)
        def _(value=value):
            body(value)


def store(out, eout, dense, expert, sem):
    copies = [pltpu.make_async_copy(out.at[i], dense.at[i], sem.at[i]) for i in range(2)]
    copies.append(pltpu.make_async_copy(eout, expert, sem.at[2]))
    for copy in copies:
        copy.start()
    for copy in copies:
        copy.wait()


def shards(grad, param, first, second, egrad, eparam, efirst, esecond):
    vmem = lambda *shape: pltpu.VMEM(shape, jnp.float32)
    block = (2, 64, 4 * T)
    out, eout = pl.pallas_call(
        kernel,
        out_shape=(vmem(2, 64, D), vmem(16, D)),
        in_specs=[pl.BlockSpec(memory_space=pltpu.HBM)] * 8,
        out_specs=(pl.BlockSpec(memory_space=pltpu.VMEM),) * 2,
        scratch_shapes=[
            vmem(4, *block), vmem(4, *block), vmem(2, 64, 8 * T), vmem(2, 64, 8 * T), vmem(*block), vmem(*block),
            vmem(16, 28 * T), vmem(16, 28 * T),
            vmem(2, *block), vmem(*block), vmem(*block), vmem(7, 64, T), vmem(64, T), vmem(7, 2, 8, 4 * T), vmem(2, 8, 4 * T), vmem(7, 8, T),
            vmem(2, 4, 2, 8, 4 * T), vmem(2, 3, 2, 8, 4 * T), vmem(2, 8, 8 * T), vmem(3, 2, 8, 2 * T), vmem(2, 8, 2 * T), vmem(7, 8, T),
            vmem(4, 64, T), vmem(3, 64, T), vmem(64, T), vmem(7, 8, T), vmem(4, 8, T),
            vmem(3, 16, 7 * T), vmem(3, 16, 7 * T), vmem(3, 2, D), vmem(4, 3, 3, 2, T), vmem(3, 3, 8, T),
            pltpu.SemaphoreType.DMA((16,)),
            pltpu.SemaphoreType.DMA((320,)),
            pltpu.SemaphoreType.DMA((320,)),
        ],
        compiler_params=pltpu.CompilerParams(
            collective_id=0, has_side_effects=True, vmem_limit_bytes=40 * 1024 * 1024
        ),
        name="reduce_update_gather",
    )(
        *(
            pltpu.with_memory_space_constraint(a, pltpu.HBM)
            for a in (grad.reshape(2, 64, D), param, first, second, egrad.reshape(16, D), eparam, efirst, esecond)
        )
    )
    dense, expert = pl.pallas_call(
        store,
        out_shape=(
            jax.ShapeDtypeStruct((2, 64, D), jnp.float32),
            jax.ShapeDtypeStruct((16, D), jnp.float32),
        ),
        in_specs=[pl.BlockSpec(memory_space=pltpu.VMEM)] * 2,
        out_specs=(pl.BlockSpec(memory_space=pltpu.HBM),) * 2,
        scratch_shapes=[pltpu.SemaphoreType.DMA((3,))],
        compiler_params=pltpu.CompilerParams(vmem_limit_bytes=16 * 1024 * 1024),
        name="store",
    )(*(pltpu.with_memory_space_constraint(a, pltpu.VMEM) for a in (out, eout)))
    return dense.reshape(128, D), expert


def solution(mesh):
    placed = (
        P("rep", "ep", None, None),
        P("ep", None),
        P("ep", None),
        P("ep", None),
        P("rep", "ep", None),
        P("ep", None),
        P("ep", None),
        P("ep", None),
    )
    return jax.shard_map(
        shards, mesh=mesh, in_specs=placed, out_specs=(P(), P("ep", None)), check_vma=False
    )
```

```python
import jax
import jax.numpy as jnp
from jax import lax
from jax.experimental import pallas as pl
from jax.experimental.pallas import tpu as pltpu
from jax.sharding import PartitionSpec as P

MESH = pl.DeviceIdType.MESH
D = 7168
T = 128
ORDER = (4, 3, 5, 2, 6, 1, 7, 0)
DIRECT = (0, 1, 2, 3, 4, 5, 6, 7)


def way(k):
    return 1 if k in (0, 1, 2, 3) else 3


class Reduce:
    def __init__(self, part, half, relays, arrived, send, peer):
        self.part, self.half, self.relays, self.arrived = part, half, relays, arrived
        self.send, self.peer = send, peer

    def start(self):
        part, half, peer, relays = self.part, self.half, self.peer, self.relays
        self.three = [self.send(part(3), relays.at[0], peer(1)), self.send(part(-3), relays.at[1], peer(7))]
        self.four = [
            self.send(half(part(4), i), half(relays.at[2], i), peer((2, 6)[i])) for i in range(2)
        ]
        self.one = [self.send(part(d), self.arrived.at[i], peer(d)) for i, d in enumerate((1, 7))]

    def relay(self):
        self.two = []
        for i, d in enumerate((2, 6)):
            mine = self.part(d)
            self.three[i].wait_recv()
            mine[...] = mine[...] + self.relays[i]
            self.four[i].wait_recv()
            more = self.half(mine, i)
            more[...] = more[...] + self.half(self.relays.at[2], i)[...]
            self.two.append(self.send(mine, self.arrived.at[2 + i], self.peer(d)))

    def finish(self):
        total = self.part(0)[...]
        for i, copy in enumerate(self.one + self.two):
            copy.wait_recv()
            total = total + self.arrived[i]
        return total


class Gather:
    def __init__(self, block, half, send, peer):
        self.block, self.half, self.send, self.peer = block, half, send, peer
        self.straight = peer.__name__ in ('z_peer',)

    def start(self):
        mine = self.block(0)
        self.all = {}
        if self.straight:
            self.all = {d: self.send(mine, mine, self.peer(d)) for d in (1, 7, 2, 6, 3, 5, 4)}
            return
        self.two = [self.send(mine, mine, self.peer(d)) for d in (2, 6)]
        self.one = [self.send(mine, mine, self.peer(d)) for d in (1, 7)]

    def forward(self):
        self.rest = []
        if self.straight:
            return
        for i, d in enumerate((2, 6)):
            self.two[i].wait_recv()
            got = self.block(-d)
            self.rest.append(self.send(got, got, self.peer((1, 7)[i])))
            self.rest.append(self.send(self.half(got, i), self.half(got, i), self.peer(d)))

    def finish(self):
        if self.straight:
            for copy in self.all.values():
                copy.wait_recv()
            return
        for copy in self.one + self.rest:
            copy.wait_recv()


def adamw(grad, param, first, second):
    first_new = 0.9 * first + (1.0 - 0.9) * grad
    second_new = 0.95 * second + (1.0 - 0.95) * grad * grad
    step_dir = first_new / 0.19 / (jnp.sqrt(second_new / 0.0975) + 1e-08)
    return param - 0.2 * (step_dir + 0.1 * param)


def tiles(start, count):
    first = start * T
    if not isinstance(first, int):
        first = pl.multiple_of(first, T)
    return pl.ds(first, count * T)


def eight(index):
    return pl.ds(pl.multiple_of(index * 8, 8), 8)


def kernel(
    grad, param, first, second, egrad, eparam, efirst, esecond,
    out, eout,
    g_a, p_a, g_c, p_c, g_b, p_b, g_e, p_e,
    r_a1, relay_a, s_a, r_a2y, t_ay, r_a2z, t_az, r_a3,
    r_c1, relay_c, s_c, r_c2, t_c, r_c3,
    r_b1, relay_b, s_b, r_b2, r_b3,
    r_e, ep_buf, state, gathered, packed,
    load_sem, send_sem, recv_sem, passed,
):
    rep, ep = lax.axis_index("rep"), lax.axis_index("ep")
    yh, yl = rep // 2, ep // 32
    core = rep - yh * 2
    rest = ep - yl * 32
    z = rest // 4
    x = rest - z * 4
    y = yh * 2 + yl

    def around(v, n):
        return [v] + [jnp.where(v + d >= n, v + d - n, v + d) for d in range(1, n)]

    xs, ys, zs = around(x, 4), around(y, 8), around(z, 8)
    yhs = [v // 2 for v in ys]
    yls = [yl, 1 - yl] * 4

    def x_peer(d):
        return {"rep": rep, "ep": ep + (xs[d] - x)}

    def y_peer(d):
        return {"rep": yhs[d] * 2 + core, "ep": ep + (yls[d] - yl) * 32}

    def z_peer(d):
        return {"rep": rep, "ep": ep + (zs[d] - z) * 4}

    partner = {"rep": rep + 1 - 2 * core, "ep": ep}

    barrier = pltpu.get_barrier_semaphore()
    near_peers = [f(d) for d in (2, 6, 1, 7) for f in (y_peer, z_peer)]
    near_peers += [x_peer(d) for d in (2, 1, 3)] + [partner]
    for peer in near_peers:
        pl.semaphore_signal(barrier, inc=1, device_id=peer, device_id_type=MESH)

    def body(c):
        n_load, n_sem = [0], [0]
        sent, flushed = [], [0]

        def load(src, dst):
            copy = pltpu.make_async_copy(src, dst, load_sem.at[n_load[0]])
            n_load[0] += 1
            copy.start()
            return copy

        def link(src, dst, device):
            k = n_sem[0]
            n_sem[0] += 1
            return pltpu.make_async_remote_copy(
                src, dst, send_sem.at[k], recv_sem.at[k], device_id=device, device_id_type=MESH
            )

        def flush():
            for copy in sent[flushed[0]:]:
                copy.wait_send()
            flushed[0] = len(sent)

        def send(src, dst, device):
            copy = link(src, dst, device)
            copy.start()
            sent.append(copy)
            return copy

        o = 1 - c
        order = [xs[d] for d in (2, 1, 3, 0)]
        own_a = [load(grad.at[:, :, tiles(c * 16 + xx * 4, 4)], g_a.at[xx]) for xx in order]
        own_c = load(grad.at[:, :, tiles(32 + c * 8, 8)], g_c)
        own_b = load(grad.at[:, :, tiles(48 + c * 4, 4)], g_b)
        own_e = load(egrad.at[:, tiles(c * 28, 28)], g_e)
        e_cols = tiles(c * 28 + yh * 7, 7)
        own_s = [load(r, state.at[i]) for i, r in enumerate((param, first, second))]
        own_ep = [load(r.at[:, e_cols], ep_buf.at[i]) for i, r in enumerate((eparam, efirst, esecond))]
        for copy in own_s:
            copy.wait()

        pl.semaphore_wait(barrier, len(near_peers))
        for peer in near_peers[:8]:
            pl.semaphore_signal(passed, inc=1, device_id=peer, device_id_type=MESH)

        def part(xx):
            return send(grad.at[:, :, tiles(o * 16 + xx * 4, 4)], p_a.at[xx], partner)

        part_a = [part(order[0])]
        part_c = send(grad.at[:, :, tiles(32 + o * 8, 8)], p_c, partner)
        part_b = send(grad.at[:, :, tiles(48 + o * 4, 4)], p_b, partner)
        part_e = send(egrad.at[:, tiles(o * 28, 28)], p_e, partner)
        part_a += [part(xx) for xx in order[1:]]

        def state_tiles(xx):
            jj = jnp.where(yh >= 2, yh - 2, yh)
            return (c * 16 + xx * 4 + yh, 32 + c * 8 + xx * 2 + jj, 48 + c * 4 + yh)

        state_recv = []
        for d in range(1, 4):
            for i, ct in enumerate(state_tiles(xs[d])):
                state_recv.append(send(state.at[:, :, tiles(ct, 1)], gathered.at[d, i], x_peer(d)))

        def piece(ref, k):
            k = k % 8
            if c == 0:
                return ref.at[yls[k], :, tiles(yhs[k], 1)]
            return ref.at[:, eight(zs[k]), :]

        def a_sum(i):
            own_a[i].wait()
            part_a[i].wait_recv()
            g_a[order[i]] = g_a[order[i]] + p_a[order[i]]

        a_sum(0)
        far = {k: send(piece(g_a.at[xs[2]], k), piece(relay_a, k), x_peer(way(k))) for k in ORDER}

        own_c.wait()
        part_c.wait_recv()
        g_c[...] = g_c[...] + p_c[...]
        ring_c = []
        for h in range(2):
            ring_c.append(
                Reduce(
                    lambda k, h=h: g_c.at[:, eight(zs[k % 8]), 4 * T * h : 4 * T * (h + 1)],
                    lambda ref, i: ref.at[i],
                    relay_c.at[h], r_c1.at[h], send, z_peer,
                )
            )
            ring_c[h].start()

        own_b.wait()
        part_b.wait_recv()
        g_b[...] = g_b[...] + p_b[...]
        ring_b = Reduce(
            lambda k: g_b.at[yls[k % 8], :, tiles(yhs[k % 8], 1)],
            lambda ref, i: ref.at[pl.ds(32 * i, 32), :],
            relay_b, r_b1, send, y_peer,
        )
        ring_b.start()

        pl.semaphore_wait(passed, 8)

        own_e.wait()
        part_e.wait_recv()
        g_e[...] = g_e[...] + p_e[...]
        e1 = [
            send(g_e.at[:, tiles(yhs[2 * d] * 7, 7)], r_e.at[d - 1], y_peer(2 * d)) for d in range(1, 4)
        ]

        a_sum(1)
        a_sum(2)
        near = {1: {}, 3: {}}
        for k in ORDER:
            d = 4 - way(k)
            near[d][k] = send(piece(g_a.at[xs[d]], k), piece(r_a1.at[d // 2], k), x_peer(d))

        for k in ORDER:
            d = way(k)
            far[k].wait_recv()
            mine = piece(g_a.at[xs[d]], k)
            mine[...] = mine[...] + piece(relay_a, k)[...]
            near[d][k] = send(mine, piece(r_a1.at[d // 2], k), x_peer(d))

        ring_c[0].relay()
        ring_c[1].relay()
        ring_b.relay()
        a_sum(3)

        for copy in state_recv:
            copy.wait_recv()
        for i, ct in enumerate(state_tiles(x)):
            for d in range(4):
                row = pl.ds(2 * xs[(4 - d) % 4], 2)
                for j in range(3):
                    if d == 0:
                        packed[i, j, row, :] = state[j, :, tiles(ct, 1)]
                    else:
                        packed[i, j, row, :] = gathered[d, i, j]

        second_a, r_a2, t_a = ([], r_a2y, t_ay) if c == 0 else ([], r_a2z, t_az)
        mid_peer, last_peer = (y_peer, z_peer) if c == 0 else (z_peer, y_peer)
        for k in ORDER:
            near[1][k].wait_recv()
            near[3][k].wait_recv()
            total = piece(g_a.at[x], k)[...] + piece(r_a1.at[0], k)[...] + piece(r_a1.at[1], k)[...]
            if k:
                piece(s_a, k)[...] = total
                second_a.append(send(piece(s_a, k), r_a2.at[k - 1], mid_peer(k)))
            else:
                t_a[...] = total

        for h in range(2):
            s_c[:, :, 4 * T * h : 4 * T * (h + 1)] = ring_c[h].finish()
        c2 = [
            send(s_c.at[:, :, tiles(2 * xs[d], 2)], r_c2.at[d - 1], x_peer(d)) for d in (2, 1, 3)
        ]

        s_b[...] = ring_b.finish()
        b2 = [send(s_b.at[eight(zs[d]), :], r_b2.at[d - 1], z_peer(d)) for d in ORDER[:7]]

        for copy in e1:
            copy.wait_recv()
        for copy in own_ep:
            copy.wait()
        total = g_e[:, tiles(yh * 7, 7)]
        for d in range(1, 4):
            total = total + r_e[d - 1]
        eout[:, e_cols] = adamw(total, ep_buf[0], ep_buf[1], ep_buf[2])

        for copy in second_a:
            copy.wait_recv()
        total = t_a[...]
        for d in range(1, 8):
            total = total + r_a2[d - 1]
        t_a[...] = total
        a3 = []
        for d in ORDER[:7]:
            if c == 0:
                src = t_a.at[eight(zs[d]), :]
            else:
                src = t_a.at[yls[d], :, tiles(yhs[d], 1)]
            a3.append(send(src, r_a3.at[d - 1], last_peer(d)))

        for copy in c2:
            copy.wait_recv()
        total = s_c[:, :, tiles(2 * x, 2)]
        for d in range(1, 4):
            total = total + r_c2[d - 1]
        t_c[...] = total
        x_odd = x - 2 * (x // 2)
        halves = [v // 2 for v in yhs]
        owner = [v == x_odd for v in halves]

        c3 = []
        for d in range(1, 8):
            copy = link(t_c.at[yls[d], :, tiles(yhs[d] - 2 * halves[d], 1)], r_c3.at[d - 1], y_peer(d))
            c3.append(copy)

            @pl.when(owner[d])
            def _(copy=copy):
                copy.start()

        for copy in b2:
            copy.wait_recv()
        total = s_b[eight(z), :]
        for d in range(1, 8):
            total = total + r_b2[d - 1]
        r_b3[x] = total
        b3 = [send(r_b3.at[x], r_b3.at[x], x_peer(d)) for d in (2, 1, 3)]

        for copy in a3:
            copy.wait_recv()
        total = t_a[eight(z), :] if c == 0 else t_a[yl, :, tiles(yh, 1)]
        for d in range(1, 8):
            total = total + r_a3[d - 1]
        ct_a, ct_c, ct_b = state_tiles(x)
        tile_a = out.at[yl, eight(z), tiles(ct_a, 1)]
        tile_a[...] = adamw(total, packed[0, 0], packed[0, 1], packed[0, 2])
        a4 = [send(tile_a, tile_a, last_peer(d)) for d in ORDER[:7]]

        tile_c = out.at[yl, eight(z), tiles(ct_c, 1)]
        c4 = [link(tile_c, tile_c, y_peer(d)) for d in range(1, 8)]
        mine_c = owner[0]

        @pl.when(mine_c)
        def _():
            for copy in c3:
                copy.wait_recv()
            total = t_c[yl, :, tiles(yh - 2 * halves[0], 1)]
            for d in range(1, 8):
                total = total + r_c3[d - 1]
            tile_c[...] = adamw(total, packed[1, 0], packed[1, 1], packed[1, 2])
            for copy in c4:
                copy.start()

        tile_b = out.at[yl, eight(z), tiles(ct_b, 1)]
        for copy in b3:
            copy.wait_recv()
        total = r_b3[0] + r_b3[1] + r_b3[2] + r_b3[3]
        tile_b[...] = adamw(total, packed[2, 0], packed[2, 1], packed[2, 2])
        b5 = [send(tile_b, tile_b, z_peer(d)) for d in ORDER[:7]]

        for d in range(1, 8):
            @pl.when(owner[d])
            def _(copy=c3[d - 1]):
                copy.wait_send()

        flush()

        done = []
        e2 = [send(eout.at[:, e_cols], eout.at[:, e_cols], y_peer(2 * d)) for d in range(1, 4)]
        done.append(send(eout.at[:, e_cols], eout.at[:, e_cols], partner))

        for copy in a4:
            copy.wait_recv()
        block_a = [out.at[:, :, tiles(c * 16 + xx * 4, 4)] for xx in xs]
        mine = piece(block_a[0], 0)
        a5 = {k: send(mine, mine, mid_peer(k)) for k in (1, 7, 2, 6, 3, 5, 4)}
        a6, a7 = {1: {}, 3: {}}, {}

        def a_out(q):
            got = piece(block_a[0], q)
            if q in DIRECT:
                a7[q] = send(got, got, x_peer(2))
            for d in (way(q), 4 - way(q)):
                a6[d][q] = send(got, got, x_peer(d))
            done.append(send(got, got, partner))

        def a_in(q):
            for d in (way(q), 4 - way(q)):
                a6[d][q].wait_recv()
                got = piece(block_a[4 - d], q)
                if q not in DIRECT and d == way(q):
                    a7[q] = send(got, got, x_peer(d))
                done.append(send(got, got, partner))

        def a_last(q):
            a7[q].wait_recv()
            got = piece(block_a[2], q)
            done.append(send(got, got, partner))

        a_out(0)

        for d in range(1, 8):
            @pl.when(owner[8 - d])
            def _(copy=c4[d - 1]):
                copy.wait_recv()
        mine = out.at[:, eight(z), tiles(32 + c * 8 + x * 2, 2)]
        c5 = {d: send(mine, mine, x_peer(d)) for d in (2, 1, 3)}
        c6 = [
            Gather(
                lambda k, xx=xx: out.at[:, eight(zs[k % 8]), tiles(32 + c * 8 + xx * 2, 2)],
                lambda ref, i: ref.at[i],
                send, z_peer,
            )
            for xx in xs
        ]
        c6[0].start()

        def c_in(d):
            c5[d].wait_recv()
            c6[4 - d].start()

        def c_last(i):
            c6[i].finish()
            got = out.at[:, :, tiles(32 + c * 8 + xs[i] * 2, 2)]
            done.append(send(got, got, partner))

        for copy in b5:
            copy.wait_recv()
        b6 = Gather(
            lambda k: out.at[yls[k % 8], :, tiles(48 + c * 4 + yhs[k % 8], 1)],
            lambda ref, i: ref.at[pl.ds(32 * i, 32), :],
            send, y_peer,
        )
        b6.start()

        def e_in(d):
            e2[d - 1].wait_recv()
            cols = tiles(c * 28 + yhs[8 - 2 * d] * 7, 7)
            done.append(send(eout.at[:, cols], eout.at[:, cols], partner))

        def a_mid(q):
            a5[8 - q].wait_recv()
            a_out(q)

        a_mid(7)
        a_mid(1)
        a_in(0)
        c_in(1)
        c_in(3)
        a_mid(6)
        a_mid(2)
        c_in(2)
        c6[0].forward()
        b6.forward()
        a_mid(5)
        a_mid(3)
        a_mid(4)
        a_in(7)
        a_in(1)
        c6[3].forward()
        c6[1].forward()
        a_last(0)
        a_in(6)
        a_in(2)
        c6[2].forward()
        b6.finish()
        got = out.at[:, :, tiles(48 + c * 4, 4)]
        done.append(send(got, got, partner))

        @pl.when(mine_c)
        def _():
            for copy in c4:
                copy.wait_send()

        a_last(7)
        a_last(1)
        e_in(1)
        e_in(2)
        e_in(3)
        c_last(0)
        a_in(5)
        a_in(3)
        a_in(4)
        c_last(3)
        c_last(1)
        a_last(6)
        a_last(2)
        a_last(5)
        a_last(3)
        a_last(4)
        c_last(2)

        flush()
        for copy in done:
            copy.wait_recv()

    for value in range(2):
        @pl.when(core == value)
        def _(value=value):
            body(value)


def store(out, eout, dense, expert, sem):
    copies = [pltpu.make_async_copy(out.at[i], dense.at[i], sem.at[i]) for i in range(2)]
    copies.append(pltpu.make_async_copy(eout, expert, sem.at[2]))
    for copy in copies:
        copy.start()
    for copy in copies:
        copy.wait()


def shards(grad, param, first, second, egrad, eparam, efirst, esecond):
    vmem = lambda *shape: pltpu.VMEM(shape, jnp.float32)
    block = (2, 64, 4 * T)
    out, eout = pl.pallas_call(
        kernel,
        out_shape=(vmem(2, 64, D), vmem(16, D)),
        in_specs=[pl.BlockSpec(memory_space=pltpu.HBM)] * 8,
        out_specs=(pl.BlockSpec(memory_space=pltpu.VMEM),) * 2,
        scratch_shapes=[
            vmem(4, *block), vmem(4, *block), vmem(2, 64, 8 * T), vmem(2, 64, 8 * T), vmem(*block), vmem(*block),
            vmem(16, 28 * T), vmem(16, 28 * T),
            vmem(2, *block), vmem(*block), vmem(*block), vmem(7, 64, T), vmem(64, T), vmem(7, 2, 8, 4 * T), vmem(2, 8, 4 * T), vmem(7, 8, T),
            vmem(2, 4, 2, 8, 4 * T), vmem(2, 3, 2, 8, 4 * T), vmem(2, 8, 8 * T), vmem(3, 2, 8, 2 * T), vmem(2, 8, 2 * T), vmem(7, 8, T),
            vmem(4, 64, T), vmem(3, 64, T), vmem(64, T), vmem(7, 8, T), vmem(4, 8, T),
            vmem(3, 16, 7 * T), vmem(3, 16, 7 * T), vmem(3, 2, D), vmem(4, 3, 3, 2, T), vmem(3, 3, 8, T),
            pltpu.SemaphoreType.DMA((16,)),
            pltpu.SemaphoreType.DMA((320,)),
            pltpu.SemaphoreType.DMA((320,)),
            pltpu.SemaphoreType.REGULAR,
        ],
        compiler_params=pltpu.CompilerParams(
            collective_id=0, has_side_effects=True, vmem_limit_bytes=40 * 1024 * 1024
        ),
        name="reduce_update_gather",
    )(
        *(
            pltpu.with_memory_space_constraint(a, pltpu.HBM)
            for a in (grad.reshape(2, 64, D), param, first, second, egrad.reshape(16, D), eparam, efirst, esecond)
        )
    )
    dense, expert = pl.pallas_call(
        store,
        out_shape=(
            jax.ShapeDtypeStruct((2, 64, D), jnp.float32),
            jax.ShapeDtypeStruct((16, D), jnp.float32),
        ),
        in_specs=[pl.BlockSpec(memory_space=pltpu.VMEM)] * 2,
        out_specs=(pl.BlockSpec(memory_space=pltpu.HBM),) * 2,
        scratch_shapes=[pltpu.SemaphoreType.DMA((3,))],
        compiler_params=pltpu.CompilerParams(vmem_limit_bytes=16 * 1024 * 1024),
        name="store",
    )(*(pltpu.with_memory_space_constraint(a, pltpu.VMEM) for a in (out, eout)))
    return dense.reshape(128, D), expert


def solution(mesh):
    placed = (
        P("rep", "ep", None, None),
        P("ep", None),
        P("ep", None),
        P("ep", None),
        P("rep", "ep", None),
        P("ep", None),
        P("ep", None),
        P("ep", None),
    )
    return jax.shard_map(
        shards, mesh=mesh, in_specs=placed, out_specs=(P(), P("ep", None)), check_vma=False
    )
```

```python
import jax
import jax.numpy as jnp
from jax import lax
from jax.experimental import pallas as pl
from jax.experimental.pallas import tpu as pltpu
from jax.sharding import PartitionSpec as P

MESH = pl.DeviceIdType.MESH
D = 7168
T = 128
ORDER = (4, 3, 5, 2, 6, 1, 7, 0)
DIRECT = (0, 1, 2, 3, 4, 5, 6, 7)


def way(k):
    return 1 if k in (0, 1, 2, 3) else 3


class Reduce:
    def __init__(self, part, half, relays, arrived, send, peer):
        self.part, self.half, self.relays, self.arrived = part, half, relays, arrived
        self.send, self.peer = send, peer

    def start(self):
        part, half, peer, relays = self.part, self.half, self.peer, self.relays
        self.three = [self.send(part(3), relays.at[0], peer(1)), self.send(part(-3), relays.at[1], peer(7))]
        self.four = [
            self.send(half(part(4), i), half(relays.at[2], i), peer((2, 6)[i])) for i in range(2)
        ]
        self.one = [self.send(part(d), self.arrived.at[i], peer(d)) for i, d in enumerate((1, 7))]

    def relay(self):
        self.two = []
        for i, d in enumerate((2, 6)):
            mine = self.part(d)
            self.three[i].wait_recv()
            mine[...] = mine[...] + self.relays[i]
            self.four[i].wait_recv()
            more = self.half(mine, i)
            more[...] = more[...] + self.half(self.relays.at[2], i)[...]
            self.two.append(self.send(mine, self.arrived.at[2 + i], self.peer(d)))

    def finish(self):
        total = self.part(0)[...]
        for i, copy in enumerate(self.one + self.two):
            copy.wait_recv()
            total = total + self.arrived[i]
        return total


class Gather:
    def __init__(self, block, half, send, peer):
        self.block, self.half, self.send, self.peer = block, half, send, peer
        self.straight = peer.__name__ in ('z_peer',)

    def start(self):
        mine = self.block(0)
        self.all = {}
        if self.straight:
            self.all = {d: self.send(mine, mine, self.peer(d)) for d in (1, 7, 2, 6, 3, 5, 4)}
            return
        self.two = [self.send(mine, mine, self.peer(d)) for d in (2, 6)]
        self.one = [self.send(mine, mine, self.peer(d)) for d in (1, 7)]

    def forward(self):
        self.rest = []
        if self.straight:
            return
        for i, d in enumerate((2, 6)):
            self.two[i].wait_recv()
            got = self.block(-d)
            self.rest.append(self.send(got, got, self.peer((1, 7)[i])))
            self.rest.append(self.send(self.half(got, i), self.half(got, i), self.peer(d)))

    def finish(self):
        if self.straight:
            for copy in self.all.values():
                copy.wait_recv()
            return
        for copy in self.one + self.rest:
            copy.wait_recv()


def adamw(grad, param, first, second):
    first_new = 0.9 * first + (1.0 - 0.9) * grad
    second_new = 0.95 * second + (1.0 - 0.95) * grad * grad
    step_dir = first_new / 0.19 / (jnp.sqrt(second_new / 0.0975) + 1e-08)
    return param - 0.2 * (step_dir + 0.1 * param)


def tiles(start, count):
    first = start * T
    if not isinstance(first, int):
        first = pl.multiple_of(first, T)
    return pl.ds(first, count * T)


def eight(index):
    return pl.ds(pl.multiple_of(index * 8, 8), 8)


def kernel(
    grad, param, first, second, egrad, eparam, efirst, esecond,
    out, eout,
    g_a, p_a, g_c, p_c, g_b, p_b, g_e, p_e,
    r_a1, relay_a, s_a, r_a2y, t_ay, r_a2z, t_az, r_a3,
    r_c1, relay_c, s_c, r_c2, t_c, r_c3,
    r_b1, relay_b, s_b, r_b2, r_b3,
    r_e, ep_buf, state, gathered, packed,
    load_sem, send_sem, recv_sem, passed,
):
    rep, ep = lax.axis_index("rep"), lax.axis_index("ep")
    yh, yl = rep // 2, ep // 32
    core = rep - yh * 2
    rest = ep - yl * 32
    z = rest // 4
    x = rest - z * 4
    y = yh * 2 + yl

    def around(v, n):
        return [v] + [jnp.where(v + d >= n, v + d - n, v + d) for d in range(1, n)]

    xs, ys, zs = around(x, 4), around(y, 8), around(z, 8)
    yhs = [v // 2 for v in ys]
    yls = [yl, 1 - yl] * 4

    def x_peer(d):
        return {"rep": rep, "ep": ep + (xs[d] - x)}

    def y_peer(d):
        return {"rep": yhs[d] * 2 + core, "ep": ep + (yls[d] - yl) * 32}

    def z_peer(d):
        return {"rep": rep, "ep": ep + (zs[d] - z) * 4}

    partner = {"rep": rep + 1 - 2 * core, "ep": ep}

    barrier = pltpu.get_barrier_semaphore()
    near_peers = [f(d) for d in (2, 6, 1, 7) for f in (y_peer, z_peer)]
    near_peers += [x_peer(d) for d in (2, 1, 3)] + [partner]
    for peer in near_peers:
        pl.semaphore_signal(barrier, inc=1, device_id=peer, device_id_type=MESH)

    def body(c):
        n_load, n_sem = [0], [0]
        sent, flushed = [], [0]

        def load(src, dst):
            copy = pltpu.make_async_copy(src, dst, load_sem.at[n_load[0]])
            n_load[0] += 1
            copy.start()
            return copy

        def link(src, dst, device):
            k = n_sem[0]
            n_sem[0] += 1
            return pltpu.make_async_remote_copy(
                src, dst, send_sem.at[k], recv_sem.at[k], device_id=device, device_id_type=MESH
            )

        def flush():
            for copy in sent[flushed[0]:]:
                copy.wait_send()
            flushed[0] = len(sent)

        def send(src, dst, device):
            copy = link(src, dst, device)
            copy.start()
            sent.append(copy)
            return copy

        o = 1 - c
        order = [xs[d] for d in (2, 1, 3, 0)]
        own_a = [load(grad.at[:, :, tiles(c * 16 + xx * 4, 4)], g_a.at[xx]) for xx in order]
        own_c = load(grad.at[:, :, tiles(32 + c * 8, 8)], g_c)
        own_b = load(grad.at[:, :, tiles(48 + c * 4, 4)], g_b)
        own_e = load(egrad.at[:, tiles(c * 28, 28)], g_e)
        e_cols = tiles(c * 28 + yh * 7, 7)
        own_s = [load(r, state.at[i]) for i, r in enumerate((param, first, second))]
        own_ep = [load(r.at[:, e_cols], ep_buf.at[i]) for i, r in enumerate((eparam, efirst, esecond))]
        for copy in own_s:
            copy.wait()

        pl.semaphore_wait(barrier, len(near_peers))
        for peer in near_peers[:8]:
            pl.semaphore_signal(passed, inc=1, device_id=peer, device_id_type=MESH)

        def part(xx):
            return send(grad.at[:, :, tiles(o * 16 + xx * 4, 4)], p_a.at[xx], partner)

        part_a = [part(order[0])]
        part_c = send(grad.at[:, :, tiles(32 + o * 8, 8)], p_c, partner)
        part_b = send(grad.at[:, :, tiles(48 + o * 4, 4)], p_b, partner)
        part_e = send(egrad.at[:, tiles(o * 28, 28)], p_e, partner)
        part_a += [part(xx) for xx in order[1:]]

        def state_tiles(xx):
            jj = jnp.where(yh >= 2, yh - 2, yh)
            return (c * 16 + xx * 4 + yh, 32 + c * 8 + xx * 2 + jj, 48 + c * 4 + yh)

        state_recv = []
        for d in range(1, 4):
            for i, ct in enumerate(state_tiles(xs[d])):
                state_recv.append(send(state.at[:, :, tiles(ct, 1)], gathered.at[d, i], x_peer(d)))

        def piece(ref, k):
            k = k % 8
            if c == 0:
                return ref.at[yls[k], :, tiles(yhs[k], 1)]
            return ref.at[:, eight(zs[k]), :]

        def a_sum(i):
            own_a[i].wait()
            part_a[i].wait_recv()
            g_a[order[i]] = g_a[order[i]] + p_a[order[i]]

        a_sum(0)
        far = {k: send(piece(g_a.at[xs[2]], k), piece(relay_a, k), x_peer(way(k))) for k in ORDER}

        own_c.wait()
        part_c.wait_recv()
        g_c[...] = g_c[...] + p_c[...]
        ring_c = []
        for h in range(2):
            ring_c.append(
                Reduce(
                    lambda k, h=h: g_c.at[:, eight(zs[k % 8]), 4 * T * h : 4 * T * (h + 1)],
                    lambda ref, i: ref.at[i],
                    relay_c.at[h], r_c1.at[h], send, z_peer,
                )
            )
            ring_c[h].start()

        own_b.wait()
        part_b.wait_recv()
        g_b[...] = g_b[...] + p_b[...]
        ring_b = Reduce(
            lambda k: g_b.at[yls[k % 8], :, tiles(yhs[k % 8], 1)],
            lambda ref, i: ref.at[pl.ds(32 * i, 32), :],
            relay_b, r_b1, send, y_peer,
        )
        ring_b.start()

        pl.semaphore_wait(passed, 8)

        own_e.wait()
        part_e.wait_recv()
        g_e[...] = g_e[...] + p_e[...]
        e1 = [
            send(g_e.at[:, tiles(yhs[2 * d] * 7, 7)], r_e.at[d - 1], y_peer(2 * d)) for d in range(1, 4)
        ]

        a_sum(1)
        a_sum(2)
        near = {1: {}, 3: {}}
        for k in ORDER:
            d = 4 - way(k)
            near[d][k] = send(piece(g_a.at[xs[d]], k), piece(r_a1.at[d // 2], k), x_peer(d))

        for k in ORDER:
            d = way(k)
            far[k].wait_recv()
            mine = piece(g_a.at[xs[d]], k)
            mine[...] = mine[...] + piece(relay_a, k)[...]
            near[d][k] = send(mine, piece(r_a1.at[d // 2], k), x_peer(d))

        ring_c[0].relay()
        ring_c[1].relay()
        ring_b.relay()
        a_sum(3)

        for copy in state_recv:
            copy.wait_recv()
        for i, ct in enumerate(state_tiles(x)):
            for d in range(4):
                row = pl.ds(2 * xs[(4 - d) % 4], 2)
                for j in range(3):
                    if d == 0:
                        packed[i, j, row, :] = state[j, :, tiles(ct, 1)]
                    else:
                        packed[i, j, row, :] = gathered[d, i, j]

        second_a, r_a2, t_a = ([], r_a2y, t_ay) if c == 0 else ([], r_a2z, t_az)
        mid_peer, last_peer = (y_peer, z_peer) if c == 0 else (z_peer, y_peer)
        for k in ORDER:
            near[1][k].wait_recv()
            near[3][k].wait_recv()
            total = piece(g_a.at[x], k)[...] + piece(r_a1.at[0], k)[...] + piece(r_a1.at[1], k)[...]
            if k:
                piece(s_a, k)[...] = total
                second_a.append(send(piece(s_a, k), r_a2.at[k - 1], mid_peer(k)))
            else:
                t_a[...] = total

        for h in range(2):
            s_c[:, :, 4 * T * h : 4 * T * (h + 1)] = ring_c[h].finish()
        c2 = [
            send(s_c.at[:, :, tiles(2 * xs[d], 2)], r_c2.at[d - 1], x_peer(d)) for d in (2, 1, 3)
        ]

        s_b[...] = ring_b.finish()
        b2 = [send(s_b.at[eight(zs[d]), :], r_b2.at[d - 1], z_peer(d)) for d in ORDER[:7]]

        for copy in second_a:
            copy.wait_recv()
        total = t_a[...]
        for d in range(1, 8):
            total = total + r_a2[d - 1]
        t_a[...] = total
        a3 = []
        for d in ORDER[:7]:
            if c == 0:
                src = t_a.at[eight(zs[d]), :]
            else:
                src = t_a.at[yls[d], :, tiles(yhs[d], 1)]
            a3.append(send(src, r_a3.at[d - 1], last_peer(d)))

        for copy in c2:
            copy.wait_recv()
        total = s_c[:, :, tiles(2 * x, 2)]
        for d in range(1, 4):
            total = total + r_c2[d - 1]
        t_c[...] = total
        x_odd = x - 2 * (x // 2)
        halves = [v // 2 for v in yhs]
        owner = [v == x_odd for v in halves]

        c3 = []
        for d in range(1, 8):
            copy = link(t_c.at[yls[d], :, tiles(yhs[d] - 2 * halves[d], 1)], r_c3.at[d - 1], y_peer(d))
            c3.append(copy)

            @pl.when(owner[d])
            def _(copy=copy):
                copy.start()

        for copy in e1:
            copy.wait_recv()
        for copy in own_ep:
            copy.wait()
        total = g_e[:, tiles(yh * 7, 7)]
        for d in range(1, 4):
            total = total + r_e[d - 1]
        eout[:, e_cols] = adamw(total, ep_buf[0], ep_buf[1], ep_buf[2])

        for copy in b2:
            copy.wait_recv()
        total = s_b[eight(z), :]
        for d in range(1, 8):
            total = total + r_b2[d - 1]
        r_b3[x] = total
        b3 = [send(r_b3.at[x], r_b3.at[x], x_peer(d)) for d in (2, 1, 3)]

        for copy in a3:
            copy.wait_recv()
        total = t_a[eight(z), :] if c == 0 else t_a[yl, :, tiles(yh, 1)]
        for d in range(1, 8):
            total = total + r_a3[d - 1]
        ct_a, ct_c, ct_b = state_tiles(x)
        tile_a = out.at[yl, eight(z), tiles(ct_a, 1)]
        tile_a[...] = adamw(total, packed[0, 0], packed[0, 1], packed[0, 2])
        a4 = [send(tile_a, tile_a, last_peer(d)) for d in ORDER[:7]]

        tile_c = out.at[yl, eight(z), tiles(ct_c, 1)]
        c4 = [link(tile_c, tile_c, y_peer(d)) for d in range(1, 8)]
        mine_c = owner[0]

        @pl.when(mine_c)
        def _():
            for copy in c3:
                copy.wait_recv()
            total = t_c[yl, :, tiles(yh - 2 * halves[0], 1)]
            for d in range(1, 8):
                total = total + r_c3[d - 1]
            tile_c[...] = adamw(total, packed[1, 0], packed[1, 1], packed[1, 2])
            for copy in c4:
                copy.start()

        tile_b = out.at[yl, eight(z), tiles(ct_b, 1)]
        for copy in b3:
            copy.wait_recv()
        total = r_b3[0] + r_b3[1] + r_b3[2] + r_b3[3]
        tile_b[...] = adamw(total, packed[2, 0], packed[2, 1], packed[2, 2])
        b5 = [send(tile_b, tile_b, z_peer(d)) for d in ORDER[:7]]

        for d in range(1, 8):
            @pl.when(owner[d])
            def _(copy=c3[d - 1]):
                copy.wait_send()

        flush()

        done = []
        e2 = [send(eout.at[:, e_cols], eout.at[:, e_cols], y_peer(2 * d)) for d in range(1, 4)]
        done.append(send(eout.at[:, e_cols], eout.at[:, e_cols], partner))

        for copy in a4:
            copy.wait_recv()
        block_a = [out.at[:, :, tiles(c * 16 + xx * 4, 4)] for xx in xs]
        mine = piece(block_a[0], 0)
        a5 = {k: send(mine, mine, mid_peer(k)) for k in (1, 7, 2, 6, 3, 5, 4)}
        a6, a7 = {1: {}, 3: {}}, {}

        def a_out(q):
            got = piece(block_a[0], q)
            if q in DIRECT:
                a7[q] = send(got, got, x_peer(2))
            for d in (way(q), 4 - way(q)):
                a6[d][q] = send(got, got, x_peer(d))
            done.append(send(got, got, partner))

        def a_in(q):
            for d in (way(q), 4 - way(q)):
                a6[d][q].wait_recv()
                got = piece(block_a[4 - d], q)
                if q not in DIRECT and d == way(q):
                    a7[q] = send(got, got, x_peer(d))
                done.append(send(got, got, partner))

        def a_last(q):
            a7[q].wait_recv()
            got = piece(block_a[2], q)
            done.append(send(got, got, partner))

        a_out(0)

        for d in range(1, 8):
            @pl.when(owner[8 - d])
            def _(copy=c4[d - 1]):
                copy.wait_recv()
        mine = out.at[:, eight(z), tiles(32 + c * 8 + x * 2, 2)]
        c5 = {d: send(mine, mine, x_peer(d)) for d in (2, 1, 3)}
        c6 = [
            Gather(
                lambda k, xx=xx: out.at[:, eight(zs[k % 8]), tiles(32 + c * 8 + xx * 2, 2)],
                lambda ref, i: ref.at[i],
                send, z_peer,
            )
            for xx in xs
        ]
        c6[0].start()

        def c_in(d):
            c5[d].wait_recv()
            c6[4 - d].start()

        def c_last(i):
            c6[i].finish()
            got = out.at[:, :, tiles(32 + c * 8 + xs[i] * 2, 2)]
            done.append(send(got, got, partner))

        for copy in b5:
            copy.wait_recv()
        b6 = Gather(
            lambda k: out.at[yls[k % 8], :, tiles(48 + c * 4 + yhs[k % 8], 1)],
            lambda ref, i: ref.at[pl.ds(32 * i, 32), :],
            send, y_peer,
        )
        b6.start()

        def e_in(d):
            e2[d - 1].wait_recv()
            cols = tiles(c * 28 + yhs[8 - 2 * d] * 7, 7)
            done.append(send(eout.at[:, cols], eout.at[:, cols], partner))

        def a_mid(q):
            a5[8 - q].wait_recv()
            a_out(q)

        a_mid(7)
        a_mid(1)
        a_in(0)
        c_in(1)
        c_in(3)
        a_mid(6)
        a_mid(2)
        c_in(2)
        c6[0].forward()
        c6[1].forward()
        c6[2].forward()
        c6[3].forward()
        b6.forward()
        a_mid(5)
        a_mid(3)
        a_mid(4)
        @pl.when(mine_c)
        def _():
            for copy in c4:
                copy.wait_send()

        a_last(0)
        a_in(7)
        a_last(7)
        a_in(1)
        a_last(1)
        e_in(1)
        e_in(2)
        e_in(3)
        b6.finish()
        got = out.at[:, :, tiles(48 + c * 4, 4)]
        done.append(send(got, got, partner))
        a_in(6)
        a_last(6)
        c_last(0)
        a_in(2)
        a_last(2)
        c_last(3)
        a_in(5)
        a_last(5)
        c_last(1)
        a_in(3)
        a_last(3)
        a_in(4)
        a_last(4)
        c_last(2)

        flush()
        for copy in done:
            copy.wait_recv()

    for value in range(2):
        @pl.when(core == value)
        def _(value=value):
            body(value)


def store(out, eout, dense, expert, sem):
    copies = [pltpu.make_async_copy(out.at[i], dense.at[i], sem.at[i]) for i in range(2)]
    copies.append(pltpu.make_async_copy(eout, expert, sem.at[2]))
    for copy in copies:
        copy.start()
    for copy in copies:
        copy.wait()


def shards(grad, param, first, second, egrad, eparam, efirst, esecond):
    vmem = lambda *shape: pltpu.VMEM(shape, jnp.float32)
    block = (2, 64, 4 * T)
    out, eout = pl.pallas_call(
        kernel,
        out_shape=(vmem(2, 64, D), vmem(16, D)),
        in_specs=[pl.BlockSpec(memory_space=pltpu.HBM)] * 8,
        out_specs=(pl.BlockSpec(memory_space=pltpu.VMEM),) * 2,
        scratch_shapes=[
            vmem(4, *block), vmem(4, *block), vmem(2, 64, 8 * T), vmem(2, 64, 8 * T), vmem(*block), vmem(*block),
            vmem(16, 28 * T), vmem(16, 28 * T),
            vmem(2, *block), vmem(*block), vmem(*block), vmem(7, 64, T), vmem(64, T), vmem(7, 2, 8, 4 * T), vmem(2, 8, 4 * T), vmem(7, 8, T),
            vmem(2, 4, 2, 8, 4 * T), vmem(2, 3, 2, 8, 4 * T), vmem(2, 8, 8 * T), vmem(3, 2, 8, 2 * T), vmem(2, 8, 2 * T), vmem(7, 8, T),
            vmem(4, 64, T), vmem(3, 64, T), vmem(64, T), vmem(7, 8, T), vmem(4, 8, T),
            vmem(3, 16, 7 * T), vmem(3, 16, 7 * T), vmem(3, 2, D), vmem(4, 3, 3, 2, T), vmem(3, 3, 8, T),
            pltpu.SemaphoreType.DMA((16,)),
            pltpu.SemaphoreType.DMA((320,)),
            pltpu.SemaphoreType.DMA((320,)),
            pltpu.SemaphoreType.REGULAR,
        ],
        compiler_params=pltpu.CompilerParams(
            collective_id=0, has_side_effects=True, vmem_limit_bytes=40 * 1024 * 1024
        ),
        name="reduce_update_gather",
    )(
        *(
            pltpu.with_memory_space_constraint(a, pltpu.HBM)
            for a in (grad.reshape(2, 64, D), param, first, second, egrad.reshape(16, D), eparam, efirst, esecond)
        )
    )
    dense, expert = pl.pallas_call(
        store,
        out_shape=(
            jax.ShapeDtypeStruct((2, 64, D), jnp.float32),
            jax.ShapeDtypeStruct((16, D), jnp.float32),
        ),
        in_specs=[pl.BlockSpec(memory_space=pltpu.VMEM)] * 2,
        out_specs=(pl.BlockSpec(memory_space=pltpu.HBM),) * 2,
        scratch_shapes=[pltpu.SemaphoreType.DMA((3,))],
        compiler_params=pltpu.CompilerParams(vmem_limit_bytes=16 * 1024 * 1024),
        name="store",
    )(*(pltpu.with_memory_space_constraint(a, pltpu.VMEM) for a in (out, eout)))
    return dense.reshape(128, D), expert


def solution(mesh):
    placed = (
        P("rep", "ep", None, None),
        P("ep", None),
        P("ep", None),
        P("ep", None),
        P("rep", "ep", None),
        P("ep", None),
        P("ep", None),
        P("ep", None),
    )
    return jax.shard_map(
        shards, mesh=mesh, in_specs=placed, out_specs=(P(), P("ep", None)), check_vma=False
    )
```
